256 devices in a mesh: outer: 8 (over y, x_lo), inner: 8 (over z), fsdp: 4 (over x_hi, core).
Axes of the slice: x: 4 (x_hi: 2, x_lo: 2; x = x_hi * 2 + x_lo), y: 4, z: 8, core: 2. Of those that a mesh axis runs over, the one named last changes fastest.
Arguments:
- hidden_in: bfloat16 [4, 8192, 2304], P('fsdp', ('outer', 'inner')), may hold values from -16 to 16
- queries: bfloat16 [4, 8192, 2048], P('fsdp', ('outer', 'inner')), may hold values from -14 to 14, as said below
- keys: bfloat16 [4, 8192, 1024], P('fsdp', ('outer', 'inner')), may hold values from -5 to 5, as said below
- values: bfloat16 [4, 8192, 1024], P('fsdp', ('outer', 'inner')), may hold values from -6 to 6
- fwd_out: bfloat16 [4, 8192, 2048], P('fsdp', ('outer', 'inner')), may hold values from -6 to 6
- out_grad: bfloat16 [4, 8192, 2048], P('fsdp', ('outer', 'inner')), may hold values from -6 to 6
- lse: float32 [4, 16, 8192], P('fsdp', None, ('outer', 'inner')), may hold values from 20 to 60, as said below
- block_order: int32 [64], replicated, may hold values from 0 to 63, each once
- doc_lengths: int32 [4, 4], P('fsdp'), may hold values from 1 to 4096, 8192 in all within a row
Outputs:
- qkv_grads: bfloat16 [4, 8192, 4096], P('fsdp', ('outer', 'inner'))
- weight_grads: bfloat16 [8, 2304, 4096], P('outer', ('inner', 'fsdp'))
The draws below stay inside these ranges and needn't reach their ends.
Inputs may be any that keep to these rules, and one draw needn't show every extreme that they name: `block_order`: each context slot holds a different block. `doc_lengths`: the documents of one sequence cover it in order; one of them spans 4096 positions. `queries`: saved from the forward pass. `keys`: saved from the forward pass. `lse`: saved from the forward pass.
All inputs are finite; a program needn't handle non-finite values.
Results may differ from the reference program's by a relative error of at most 0.02.
Values may be sent and summed in bfloat16 or wider, within the bound.
A program may use at most 128 MiB of HBM per device.

```python
import math
import jax
import jax.numpy as jnp
import numpy as np
from jax import lax

D = 2304
HQ = 16
HK = 8
HD = 128
TOK_DEV = 128
NDOCS = 4
BLOCKS = 64
LENGTH = 8192
COLS = 4096
N_OUTER = 8
N_INNER = 8
N_FSDP = 4


def score_plan(key, lowest, highest):
    sign_key = jax.random.fold_in(key, 101)
    centre_key = jax.random.fold_in(key, 102)
    sign_table = jax.random.randint(sign_key, (N_FSDP, HK, HD), 0, 2).astype(jnp.float32) * 2.0 - 1.0
    centres = jax.random.uniform(centre_key, (N_FSDP, LENGTH, HQ), jnp.float32, lowest, highest)
    return (sign_table, centres)


def draw_queries(key, part):
    shape = (N_FSDP, LENGTH, HQ, HD)
    sign_table, centres = score_plan(key, 20.0, 70.0)
    key = jax.random.fold_in(key, 1)
    jitter = jnp.clip(jax.random.normal(key, shape, jnp.float32), -4.0, 4.0)
    repeated = jnp.repeat(sign_table, HQ // HK, axis=1)
    spread = 12.0 * centres / HD
    full = spread[..., None] * repeated[:, None, :, :] + 1.5 * jitter
    return full.reshape(N_FSDP, LENGTH, HQ * HD).astype(jnp.bfloat16)


def draw_keys(key, part):
    shape = (N_FSDP, LENGTH, HK, HD)
    sign_table, centres = score_plan(key, 20.0, 70.0)
    key = jax.random.fold_in(key, 2)
    jitter = jnp.clip(jax.random.normal(key, shape, jnp.float32), -4.0, 4.0)
    full = sign_table[:, None, :, :] + jitter
    return full.reshape(N_FSDP, LENGTH, HK * HD).astype(jnp.bfloat16)


def draw_lse(key, part):
    sign_table, centres = score_plan(key, 20.0, 70.0)
    key = jax.random.fold_in(key, 3)
    offset = jax.random.uniform(key, (N_FSDP, HQ, LENGTH), jnp.float32, 1.0, 3.0)
    capped = 50.0 * jnp.tanh(centres / 50.0)
    return (capped.transpose(0, 2, 1) + offset + math.log(2.0 * TOK_DEV)).astype(jnp.float32)


def with_spikes(result, rng, source, target, parts, factor):
    def block_of(dim):
        return (jnp.arange(result.shape[dim]) // (result.shape[dim] // parts)).reshape((-1,) + (1,) * (result.ndim - 1 - dim))

    one_side = jax.random.permutation(rng, parts)[block_of(target)]
    far = (block_of(target) + parts // 2) % parts
    return jnp.where((block_of(source) == one_side) | (block_of(source) == far), factor * result, result)


def level_of(own_key, extent, pieces, low, top_value):
    def one(position, parts):
        draws = jax.random.uniform(jax.random.fold_in(jax.random.fold_in(own_key, 6), position), (parts,), jnp.float32, low / len(pieces), top_value / len(pieces))
        return jnp.repeat(jnp.exp(draws), extent[position] // parts).reshape((-1,) + (1,) * (len(extent) - position - 1))

    factor_of = one(*pieces[0])
    for cut in pieces[1:]:
        factor_of = factor_of * one(*cut)
    return factor_of


def split_up(count, total, bound, skew):
    loads = [(1 << 20) // math.isqrt(rank ** skew) + 1 for rank in range(2, count + 1)]
    rest, counts = total - bound - (count - 1), [1] * (count - 1)
    while rest > 0:
        movable = [i for i in range(count - 1) if counts[i] < bound]
        mass, budget = sum([loads[i] for i in movable]), rest
        for i in movable:
            addition = min(bound - counts[i], max(1, budget * loads[i] // mass), rest)
            counts[i] = counts[i] + addition
            rest = rest - addition
    return np.array([bound] + counts)


def uneven(stream_key, count, total, most, lean):
    if count == 2:
        one = jax.random.randint(stream_key, (), max(1, total - most), min(most, total - 1) + 1)
        return jnp.stack([one, total - one])
    sizes = jnp.asarray(split_up(count, total, most, lean), jnp.int32)
    couples = (count - 1) // 2
    source_of, taker = sizes[1:1 + 2 * couples:2], sizes[2:2 + 2 * couples:2]
    slack = jnp.minimum(source_of - 1, most - taker)
    shifted = jax.random.randint(jax.random.fold_in(stream_key, 1), (couples,), 0, 1 << 20) % (slack + 1)
    sizes = sizes.at[1:1 + 2 * couples:2].set(source_of - shifted).at[2:2 + 2 * couples:2].set(taker + shifted)
    return sizes[jax.random.permutation(jax.random.fold_in(stream_key, 2), count)]


def bell_draw(stream_key, shape, scale, limit, split=(), kind=jnp.bfloat16):
    result = scale * jax.random.normal(stream_key, shape, jnp.float32)
    if split:
        result = result * level_of(stream_key, shape, split, -0.22, 0.18)
    return jnp.clip(result, -limit, limit).astype(kind)


def heavy_noise(own_key, dims, scale, limit, pieces, heavy, kind=jnp.bfloat16):
    entries = scale * jax.random.normal(own_key, dims, jnp.float32)
    if pieces:
        entries = entries * level_of(own_key, dims, pieces, -0.22, 0.18)
    return jnp.clip(with_spikes(entries, jax.random.fold_in(own_key, 3), *heavy), -limit, limit).astype(kind)


def setup_inputs(seed: int = 0) -> dict:
    arg_keys = jax.random.split(jax.random.key(seed), 10)
    return {
        "hidden_in": heavy_noise(arg_keys[0], (N_FSDP, LENGTH, D), 1.0, 16.0, ((0, 4), (1, 64)), (1, 2, 64, 4.0)),
        "queries": draw_queries(jax.random.fold_in(arg_keys[9], 71), 0),
        "keys": draw_keys(jax.random.fold_in(arg_keys[9], 71), 0),
        "values": bell_draw(arg_keys[3], (N_FSDP, LENGTH, HK * HD), 1.0, 6.0, ((0, 4), (1, 64))),
        "fwd_out": bell_draw(arg_keys[4], (N_FSDP, LENGTH, HQ * HD), 1.0, 6.0, ((0, 4), (1, 64))),
        "out_grad": bell_draw(arg_keys[5], (N_FSDP, LENGTH, HQ * HD), 1.0, 6.0, ((0, 4), (1, 64))),
        "lse": draw_lse(jax.random.fold_in(arg_keys[9], 71), 0),
        "block_order": jax.random.permutation(arg_keys[7], BLOCKS).astype(jnp.int32),
        "doc_lengths": jax.vmap(lambda own: uneven(own, NDOCS, LENGTH, LENGTH // 2, 2))(jax.random.split(arg_keys[8], N_FSDP)).reshape((N_FSDP, NDOCS)).astype(jnp.int32),
    }


softcap = 50.0
query_scale = 144.0 ** -0.5


def pair_grads(items):
    qb, kb, vb, dob, lse_b, delta_b, qpos, kpos, qdoc, kdoc = items
    tok = qb.shape[0]
    groups = HQ // HK
    qf = qb.astype(jnp.float32).reshape(tok, HK, groups, HD)
    kf = kb.astype(jnp.float32).reshape(tok, HK, HD)
    vf = vb.astype(jnp.float32).reshape(tok, HK, HD)
    dof = dob.astype(jnp.float32).reshape(tok, HK, groups, HD)
    raw = jnp.einsum("qhgd,khd->hgqk", qf, kf) * query_scale
    capped = jnp.tanh(raw / softcap)
    live = (kpos[None, :] <= qpos[:, None]) & (kdoc[None, :] == qdoc[:, None])
    prob = jnp.where(live[None, None], jnp.exp(softcap * capped - lse_b[:, :, :, None]), jnp.float32(0.0))
    prob_b = prob.astype(jnp.bfloat16)
    dprob = jnp.einsum("qhgd,khd->hgqk", dof, vf)
    dscore = (prob * (dprob - delta_b[:, :, :, None]) * (1.0 - capped * capped) * query_scale).astype(jnp.bfloat16)
    dsf = dscore.astype(jnp.float32)
    dq = jnp.einsum("hgqk,khd->qhgd", dsf, kf).reshape(tok, HQ * HD)
    dk = jnp.einsum("hgqk,qhgd->khd", dsf, qf).reshape(tok, HK * HD)
    dv = jnp.einsum("hgqk,qhgd->khd", prob_b.astype(jnp.float32), dof).reshape(tok, HK * HD)
    return dq, dk, dv


def rope_back(grad, pos, heads):
    tok = grad.shape[0]
    half = HD // 2
    g = grad.reshape(tok, heads, HD)
    inv = 10000.0 ** (-2.0 * jnp.arange(half).astype(jnp.float32) / HD)
    angle = pos.astype(jnp.float32)[:, None] * inv[None, :]
    cosv = jnp.cos(angle)[:, None, :]
    sinv = jnp.sin(angle)[:, None, :]
    g1 = g[:, :, :half]
    g2 = g[:, :, half:]
    return jnp.concatenate([g1 * cosv + g2 * sinv, g2 * cosv - g1 * sinv], axis=-1).reshape(tok, heads * HD)


def reference(hidden_in, queries, keys, values, fwd_out, out_grad, lse, block_order, doc_lengths):
    groups = HQ // HK
    nblk = N_OUTER * N_INNER
    offsets = ((0, 0), (1, 1), (1, 2), (0, 1))
    order = block_order.reshape(N_OUTER, N_INNER)
    qpos = order[:, :, None] * TOK_DEV + jnp.arange(TOK_DEV, dtype=jnp.int32)[None, None, :]
    all_grads = []
    for seq in range(N_FSDP):
        def grid(a):
            return a.reshape(N_OUTER, N_INNER, TOK_DEV, a.shape[-1])
        qg = grid(queries[seq])
        kg = grid(keys[seq])
        vg = grid(values[seq])
        dog = grid(out_grad[seq])
        lse_g = lse[seq].reshape(HK, groups, N_OUTER, N_INNER, TOK_DEV).transpose(2, 3, 0, 1, 4)
        delta = (out_grad[seq].astype(jnp.float32) * fwd_out[seq].astype(jnp.float32))
        delta = delta.reshape(N_OUTER, N_INNER, TOK_DEV, HK, groups, HD).sum(-1).transpose(0, 1, 3, 4, 2)
        lengths = doc_lengths[seq]
        starts = jnp.cumsum(lengths) - lengths
        qdoc = jnp.sum((qpos[..., None] >= starts).astype(jnp.int32), axis=-1)
        dq_sum = jnp.zeros((N_OUTER, N_INNER, TOK_DEV, HQ * HD), jnp.float32)
        dk_sum = jnp.zeros((N_OUTER, N_INNER, TOK_DEV, HK * HD), jnp.float32)
        dv_sum = jnp.zeros((N_OUTER, N_INNER, TOK_DEV, HK * HD), jnp.float32)
        for axis, shift in offsets:
            def moved(a):
                return jnp.roll(a, shift, axis=axis)

            def flat(a):
                return a.reshape((nblk,) + a.shape[2:])

            items = (flat(qg), flat(moved(kg)), flat(moved(vg)), flat(dog), flat(lse_g), flat(delta),
                     flat(qpos), flat(moved(qpos)), flat(qdoc), flat(moved(qdoc)))
            dq, dk, dv = lax.map(pair_grads, items)
            dq_sum = dq_sum + dq.reshape(dq_sum.shape)
            dk_sum = dk_sum + jnp.roll(dk.reshape(dk_sum.shape), -shift, axis=axis)
            dv_sum = dv_sum + jnp.roll(dv.reshape(dv_sum.shape), -shift, axis=axis)
        pos_flat = qpos.reshape(nblk * TOK_DEV)
        dq_pre = rope_back(dq_sum.reshape(nblk * TOK_DEV, HQ * HD), pos_flat, HQ)
        dk_pre = rope_back(dk_sum.reshape(nblk * TOK_DEV, HK * HD), pos_flat, HK)
        grads = jnp.concatenate([dq_pre, dk_pre, dv_sum.reshape(nblk * TOK_DEV, HK * HD)], axis=1).astype(jnp.bfloat16)
        all_grads.append(grads)
    qkv_grads = jnp.stack(all_grads)

    def add_term(acc, items):
        xb, gb, outer_at = items
        term = lax.dot_general(xb, gb, (((0,), (0,)), ((), ())), preferred_element_type=jnp.float32)
        rounded = lax.optimization_barrier(term.astype(jnp.bfloat16)).astype(jnp.float32)
        return acc.at[outer_at].add(rounded), None

    acc = jnp.zeros((N_OUTER, D, COLS), jnp.float32)
    outer_ids = (jnp.arange(nblk, dtype=jnp.int32) // N_INNER).astype(jnp.int32)
    for seq in range(N_FSDP):
        xs = (hidden_in[seq].reshape(nblk, TOK_DEV, D), qkv_grads[seq].reshape(nblk, TOK_DEV, COLS), outer_ids)
        acc, unused = lax.scan(add_term, acc, xs)
    return qkv_grads, acc.astype(jnp.bfloat16)
```

```python
import functools

import jax
import jax.numpy as jnp
import numpy as np
from jax import lax
from jax.experimental import pallas as pl
from jax.experimental.pallas import tpu as pltpu
from jax.sharding import PartitionSpec as P

MESH = pl.DeviceIdType.MESH
F32 = jnp.float32
BF16 = jnp.bfloat16

HQ = 16
HK = 8
HD = 128
TOK = 128
D = 2304
COLS = 4096
RING = 8
QUAD = 4
GROUPS = 4
ROWS = D // RING // 2
HALF = 512
DEAD = -1e30

CHUNKS = ((0, 512), (2048, 3072), (1024, 1536), (2560, 3584))
DQ0, DKV0, DQ1, DKV1 = 0, 1, 2, 3


def nt(a, b):
    return lax.dot_general(a, b, (((1,), (1,)), ((), ())), preferred_element_type=F32)


def tn(a, b):
    return lax.dot_general(a, b, (((0,), (0,)), ((), ())), preferred_element_type=F32)


def nn(a, b):
    return jnp.dot(a, b, preferred_element_type=F32)


def kernel(
    hid, q, k, v, fo, do, lse, order, lengths, inv,
    gout, wout,
    kvr, bias, cosf, sinf, delta, dq_acc, home, one_part,
    two_send, two_recv, car_send, car_recv, pri_send, pri_recv,
    g, xt, xt_core, xt_far, gq, part, rs_send, rs_recv, fin, fin_send, fin_recv,
    kv_s, kv_r, ret_s, ret_r, xt_s, xt_r, gx_s, gx_r, rs_ss, rs_rs, fin_s, fin_r,
):
    z = lax.axis_index("inner")
    oo = lax.axis_index("outer")
    f = lax.axis_index("fsdp")
    xh = f // 2
    c = f % 2
    up = {"inner": (z + 1) % RING}
    down = {"inner": (z + RING - 1) % RING}
    n_outer = lax.axis_size("outer")
    nxt = {"outer": (oo + 1) % n_outer}
    prv = {"outer": (oo + n_outer - 1) % n_outer}
    core = {"fsdp": xh * 2 + 1 - c}
    far = {"fsdp": (1 - xh) * 2 + c}

    sends = []

    def send(src, dst, ss, rs, to):
        cp = pltpu.make_async_remote_copy(
            src_ref=src, dst_ref=dst, send_sem=ss, recv_sem=rs, device_id=to, device_id_type=MESH
        )
        cp.start()
        sends.append(cp)
        return cp

    barrier = pltpu.get_barrier_semaphore()
    for to in (up, down, nxt, prv, core, far):
        pl.semaphore_signal(barrier, inc=1, device_id=to, device_id_type=MESH)
    pl.semaphore_wait(barrier, 6)

    cp_one, cp_two, cp_pri = {}, {}, {}
    for gi in range(GROUPS):
        cols = pl.ds(gi * 256, 256)
        for j, ref in enumerate((k, v)):
            cp_one[gi, j] = send(
                ref.at[:, cols], kvr.at[0, j, :, cols], kv_s.at[0, gi, j], kv_r.at[0, gi, j], up
            )
        for j, ref in enumerate((k, v)):
            cp_pri[gi, j] = send(
                ref.at[:, cols], kvr.at[2, j, :, cols], kv_s.at[2, gi, j], kv_r.at[2, gi, j], nxt
            )

    def forward(gi):
        cols = pl.ds(gi * 256, 256)
        for j in range(2):
            cp_one[gi, j].wait_recv()
            cp_two[gi, j] = send(
                kvr.at[0, j, :, cols], kvr.at[1, j, :, cols], kv_s.at[1, gi, j], kv_r.at[1, gi, j], up
            )

    turned = hid[...].T
    for i in range(2 * RING):
        xt[i // 2, i % 2] = turned[i * ROWS : (i + 1) * ROWS]
    cp_xc = send(xt, xt_core, xt_s.at[0], xt_r.at[0], core)
    cp_xf = send(xt.at[:, 1 - xh], xt_far.at[0], xt_s.at[1], xt_r.at[1], far)

    rows_i = lax.broadcasted_iota(jnp.int32, (TOK, TOK), 0)
    cols_i = lax.broadcasted_iota(jnp.int32, (TOK, TOK), 1)
    starts = [jnp.int32(0)]
    for i in range(3):
        starts.append(starts[-1] + lengths[0, i])

    def doc_of(pos):
        total = jnp.zeros(pos.shape, jnp.int32)
        for s in starts:
            total = total + (pos >= s).astype(jnp.int32)
        return total

    def block(outer_pos, inner_pos):
        return order[(outer_pos % n_outer) * RING + inner_pos % RING] * TOK

    qpos = block(oo, z) + cols_i
    qdoc = doc_of(qpos)
    slots = ((oo, z), (oo, z + RING - 1), (oo, z + RING - 2), (oo + n_outer - 1, z))
    for i, (a, b) in enumerate((slots[0], slots[1], slots[3], slots[2])):
        kpos = block(a, b) + rows_i
        live = (kpos <= qpos) & (doc_of(kpos) == qdoc)
        bias[i] = jnp.where(live, F32(0.0), F32(DEAD))
    angle = (block(oo, z) + rows_i).astype(F32) * inv[0:1, :]
    cosf[...] = jnp.cos(angle)
    sine = jnp.sin(angle)
    sinf[...] = jnp.where(cols_i < HD // 2, sine, -sine)

    def unrotate(grad):
        return grad * cosf[...] + pltpu.roll(grad, HD // 2, 1) * sinf[...]

    ones = jnp.ones((8, HD), BF16)
    for h in range(HQ):
        cols = slice(h * HD, (h + 1) * HD)
        prod = do[:, cols].astype(F32) * fo[:, cols].astype(F32)
        hi = prod.astype(BF16)
        lo = (prod - hi.astype(F32)).astype(BF16)
        delta[h : h + 1] = (nt(ones, hi) + nt(ones, lo))[0:1]

    cp_xc.wait_recv()
    cp_xd = send(xt_core.at[:, 1 - xh], xt_far.at[1], xt_s.at[2], xt_r.at[2], far)

    def attend(h, kk, vv, bb):
        a, b = slice(2 * h * HD, (2 * h + 1) * HD), slice((2 * h + 1) * HD, (2 * h + 2) * HD)
        qs = jnp.concatenate([q[:, a], q[:, b]], axis=0)
        dos = jnp.concatenate([do[:, a], do[:, b]], axis=0)
        lse_h = jnp.concatenate([lse[2 * h : 2 * h + 1], lse[2 * h + 1 : 2 * h + 2]], axis=1)
        delta_h = jnp.concatenate([delta[2 * h : 2 * h + 1], delta[2 * h + 1 : 2 * h + 2]], axis=1)
        capped = jnp.tanh(nt(kk, qs) * F32(1.0 / 600.0))
        prob = jnp.exp(F32(50.0) * capped - lse_h + jnp.concatenate([bb, bb], axis=1))
        dprob = nt(vv, dos)
        ds = (prob * (dprob - delta_h) * (F32(1.0 / 12.0) - F32(1.0 / 12.0) * (capped * capped))).astype(BF16)
        return tn(ds, kk), nn(ds, qs), nn(prob.astype(BF16), dos)

    def first(gi):
        for hh in range(2):
            h = gi * 2 + hh
            cols = slice(h * HD, (h + 1) * HD)
            kk = jnp.concatenate([k[:, cols], kvr[0, 0, :, cols], kvr[2, 0, :, cols]], axis=0)
            vv = jnp.concatenate([v[:, cols], kvr[0, 1, :, cols], kvr[2, 1, :, cols]], axis=0)
            dq, dk, dv = attend(h, kk, vv, bias[0:3].reshape(3 * TOK, TOK))
            dq_acc[h] = dq
            for j, val in enumerate((dk, dv)):
                home[gi, hh, j] = val[0:TOK]
                one_part[gi, hh, j] = val[TOK : 2 * TOK]
                pri_send[gi, hh, j] = val[2 * TOK : 3 * TOK].astype(BF16)

    def second(gi):
        for hh in range(2):
            h = gi * 2 + hh
            cols = slice(h * HD, (h + 1) * HD)
            dq, dk, dv = attend(h, kvr[1, 0, :, cols], kvr[1, 1, :, cols], bias[3])
            for j, val in enumerate((dk, dv)):
                two_send[gi, hh, j] = val.astype(BF16)
            total = dq_acc[h] + dq
            for i in range(2):
                g[:, (2 * h + i) * HD : (2 * h + i + 1) * HD] = unrotate(total[i * TOK : (i + 1) * TOK]).astype(BF16)

    cp_ret = {}

    def do_first(gi):
        forward(gi)
        for j in range(2):
            cp_pri[gi, j].wait_recv()
        first(gi)
        cp_ret["pri", gi] = send(pri_send.at[gi], pri_recv.at[gi], ret_s.at[0, gi], ret_r.at[0, gi], prv)

    def do_second(gi):
        for j in range(2):
            cp_two[gi, j].wait_recv()
        second(gi)
        cp_ret["two", gi] = send(two_send.at[gi], two_recv.at[gi], ret_s.at[1, gi], ret_r.at[1, gi], down)

    def carry(gi):
        cp_ret["two", gi].wait_recv()
        car_send[gi] = (two_recv[gi].astype(F32) + one_part[gi]).astype(BF16)
        cp_ret["car", gi] = send(car_send.at[gi], car_recv.at[gi], ret_s.at[2, gi], ret_r.at[2, gi], down)

    def settle(gi):
        cp_ret["car", gi].wait_recv()
        cp_ret["pri", gi].wait_recv()
        for hh in range(2):
            h = gi * 2 + hh
            dk, dv = [
                home[gi, hh, j] + car_recv[gi, hh, j].astype(F32) + pri_recv[gi, hh, j].astype(F32)
                for j in range(2)
            ]
            at = HQ * HD + h * HD
            g[:, at : at + HD] = unrotate(dk).astype(BF16)
            at = (HQ + HK) * HD + h * HD
            g[:, at : at + HD] = dv.astype(BF16)

    cp_gx = {}

    def base(ch, who):
        lo, hi = CHUNKS[ch]
        return pl.ds(pl.multiple_of(lo + who * (hi - lo), HALF), HALF)

    def swap(ch):
        mine = g.at[:, base(ch, c)]
        cp_gx[ch, 0] = send(g.at[:, base(ch, 1 - c)], gq.at[ch, 1], gx_s.at[ch, 0], gx_r.at[ch, 0], core)
        cp_gx[ch, 1] = send(mine, gq.at[ch, 2], gx_s.at[ch, 1], gx_r.at[ch, 1], far)
        gq[ch, 0] = mine[...]

    def swap_on(ch):
        cp_gx[ch, 0].wait_recv()
        cp_gx[ch, 2] = send(gq.at[ch, 1], gq.at[ch, 3], gx_s.at[ch, 2], gx_r.at[ch, 2], far)

    chains = ((0, 1, 4), (0, -1, 3), (1, -1, 4), (1, 1, 3))
    cp_rs = {}

    def term(ch, chain, step):
        half, way, hops = chains[chain]
        at = (z + 2 * RING + way * (hops - step)) % RING
        return part[ch, at, :, half * 256 : (half + 1) * 256]

    def hop(ch, chain, step, val):
        rs_send[ch, chain, step] = val.astype(BF16)
        cp_rs[ch, chain, step] = send(
            rs_send.at[ch, chain, step], rs_recv.at[ch, chain, step],
            rs_ss.at[ch, chain, step], rs_rs.at[ch, chain, step],
            up if chains[chain][1] > 0 else down,
        )

    def multiply(ch):
        cp_gx[ch, 1].wait_recv()
        cp_gx[ch, 2].wait_recv()
        for half in range(2):
            gs = gq[ch, :, :, half * 256 : (half + 1) * 256].reshape(QUAD * TOK, 256)
            for piece in range(2):
                at = slice(piece * 4, piece * 4 + 4)
                xs = jnp.concatenate(
                    [xt_mine[at], xt_mate[at], xt_far[0, at], xt_far[1, at]], axis=-1
                ).reshape(4 * ROWS, QUAD * TOK)
                part[ch, at, :, half * 256 : (half + 1) * 256] = nn(xs, gs).reshape(4, ROWS, 256)
        for chain in range(4):
            hop(ch, chain, 0, term(ch, chain, 0))

    def step(ch, s):
        for chain in range(4):
            if s < chains[chain][2]:
                cp_rs[ch, chain, s - 1].wait_recv()
                hop(ch, chain, s, rs_recv[ch, chain, s - 1].astype(F32) + term(ch, chain, s))

    def finish(ch):
        for half in range(2):
            val = part[ch, z, :, half * 256 : (half + 1) * 256]
            for chain in range(4):
                if chains[chain][0] == half:
                    last = chains[chain][2] - 1
                    cp_rs[ch, chain, last].wait_recv()
                    val = val + rs_recv[ch, chain, last].astype(F32)
            fin[ch, 0, :, half * 256 : (half + 1) * 256] = val[0 : ROWS // 2]
            fin[ch, 1, :, half * 256 : (half + 1) * 256] = val[ROWS // 2 :]
        fin_send[ch] = fin[ch, 1 - c].astype(BF16)
        cp_gx[ch, "fin"] = send(fin_send.at[ch], fin_recv.at[ch], fin_s.at[ch], fin_r.at[ch], core)
        wout[:, base(ch, c)] = fin[ch, c].astype(BF16)

    def last(ch):
        cp_gx[ch, "fin"].wait_recv()
        wout[:, base(ch, 1 - c)] = fin_recv[ch]

    xt_mine = xt.at[:, xh]
    xt_mate = xt_core.at[:, xh]

    for gi in range(GROUPS):
        do_first(gi)
    do_second(0)
    do_second(1)
    swap(DQ0)
    carry(0)
    do_second(2)
    carry(1)
    swap_on(DQ0)
    do_second(3)
    swap(DQ1)
    settle(0)
    settle(1)
    swap(DKV0)
    carry(2)
    swap_on(DQ1)
    carry(3)
    cp_xf.wait_recv()
    cp_xd.wait_recv()
    multiply(DQ0)
    swap_on(DKV0)
    settle(2)
    settle(3)
    swap(DKV1)
    step(DQ0, 1)
    multiply(DQ1)
    swap_on(DKV1)
    multiply(DKV0)
    step(DQ0, 2)
    step(DQ1, 1)
    step(DKV0, 1)
    multiply(DKV1)
    step(DQ0, 3)
    step(DQ1, 2)
    step(DKV0, 2)
    step(DKV1, 1)
    finish(DQ0)
    step(DQ1, 3)
    step(DKV0, 3)
    step(DKV1, 2)
    gout[...] = g[...]
    finish(DQ1)
    finish(DKV0)
    step(DKV1, 3)
    last(DQ0)
    last(DQ1)
    last(DKV0)
    finish(DKV1)
    last(DKV1)
    for cp in sends:
        cp.wait_send()


def local(hidden_in, queries, keys, values, fwd_out, out_grad, lse, block_order, doc_lengths):
    freq = 10000.0 ** (-2.0 * np.arange(HD // 2, dtype=np.float32) / HD)
    inv = jnp.asarray(np.broadcast_to(np.concatenate([freq, freq])[None, :], (8, HD)).astype(np.float32))
    vm = pl.BlockSpec(memory_space=pltpu.VMEM)
    sm = pl.BlockSpec(memory_space=pltpu.SMEM)
    ret = pltpu.VMEM((GROUPS, 2, 2, TOK, HD), BF16)
    dma = pltpu.SemaphoreType.DMA
    qkv, weights = pl.pallas_call(
        kernel,
        out_shape=(
            jax.ShapeDtypeStruct((TOK, COLS), BF16),
            jax.ShapeDtypeStruct((ROWS // 2, COLS), BF16),
        ),
        in_specs=[vm] * 7 + [sm, sm, vm],
        out_specs=(vm, vm),
        scratch_shapes=[
            pltpu.VMEM((3, 2, TOK, HK * HD), BF16),
            pltpu.VMEM((4, TOK, TOK), F32),
            pltpu.VMEM((TOK, HD), F32),
            pltpu.VMEM((TOK, HD), F32),
            pltpu.VMEM((HQ, TOK), F32),
            pltpu.VMEM((HK, 2 * TOK, HD), F32),
            pltpu.VMEM((GROUPS, 2, 2, TOK, HD), F32),
            pltpu.VMEM((GROUPS, 2, 2, TOK, HD), F32),
            ret, ret, ret, ret, ret, ret,
            pltpu.VMEM((TOK, COLS), BF16),
            pltpu.VMEM((RING, 2, ROWS, TOK), BF16),
            pltpu.VMEM((RING, 2, ROWS, TOK), BF16),
            pltpu.VMEM((2, RING, ROWS, TOK), BF16),
            pltpu.VMEM((4, QUAD, TOK, HALF), BF16),
            pltpu.VMEM((4, RING, ROWS, HALF), F32),
            pltpu.VMEM((4, 4, 4, ROWS, 256), BF16),
            pltpu.VMEM((4, 4, 4, ROWS, 256), BF16),
            pltpu.VMEM((4, 2, ROWS // 2, HALF), F32),
            pltpu.VMEM((4, ROWS // 2, HALF), BF16),
            pltpu.VMEM((4, ROWS // 2, HALF), BF16),
            dma((3, GROUPS, 2)), dma((3, GROUPS, 2)),
            dma((3, GROUPS)), dma((3, GROUPS)),
            dma((3,)), dma((3,)),
            dma((4, 3)), dma((4, 3)),
            dma((4, 4, 4)), dma((4, 4, 4)),
            dma((4,)), dma((4,)),
        ],
        compiler_params=pltpu.CompilerParams(
            collective_id=0, has_side_effects=True, vmem_limit_bytes=58 * 1024 * 1024
        ),
        cost_estimate=pl.CostEstimate(flops=4 * 10**9, bytes_accessed=6 * 10**6, transcendentals=2 * 10**6),
    )(
        hidden_in[0], queries[0], keys[0], values[0], fwd_out[0], out_grad[0], lse[0],
        block_order, doc_lengths, inv,
    )
    return (qkv[None], weights[None])


def solution(mesh):
    tokens = P("fsdp", ("outer", "inner"), None)
    in_specs = (tokens,) * 6 + (P("fsdp", None, ("outer", "inner")), P(), P("fsdp", None))
    out_specs = (tokens, P("outer", ("inner", "fsdp"), None))
    return jax.shard_map(local, mesh=mesh, in_specs=in_specs, out_specs=out_specs, check_vma=False)
```

```python
import functools

import jax
import jax.numpy as jnp
import numpy as np
from jax import lax
from jax.experimental import pallas as pl
from jax.experimental.pallas import tpu as pltpu
from jax.sharding import PartitionSpec as P

MESH = pl.DeviceIdType.MESH
F32 = jnp.float32
BF16 = jnp.bfloat16

HQ = 16
HK = 8
HD = 128
TOK = 128
D = 2304
COLS = 4096
RING = 8
QUAD = 4
GROUPS = 4
ROWS = D // RING // 2
HALF = 256
DEAD = -1e30

CHUNKS = tuple((512 * i, 512 * i + 256) for i in range(4)) + tuple(
    (2048 + 256 * i, 3072 + 256 * i) for i in range(4)
)
LONG_UP = ((1, 4), (-1, 3))
LONG_DOWN = ((1, 3), (-1, 4))
CHAINS = (LONG_UP, LONG_DOWN, LONG_UP, LONG_UP, LONG_DOWN, LONG_UP, LONG_UP, LONG_UP)
ORDER = (
    ("pri", 0), ("pri", 2), ("one", 2), ("turn",), ("prep",), ("one", 0), ("fwd", 2), ("first", 2), ("fwd", 0),
    ("first", 0), ("second", 2), ("swap", 2), ("relay", 2), ("one", 1), ("pri", 1), ("second", 0), ("swap", 0),
    ("xon",), ("relay", 0), ("carry", 2), ("xready",), ("fwd", 1), ("first", 1), ("one", 3), ("carry", 0), ("pri", 3),
    ("mult", 2), ("settle", 2), ("swap", 6), ("second", 1), ("relay", 6), ("swap", 1), ("relay", 1), ("fwd", 3),
    ("first", 3), ("settle", 0), ("swap", 4), ("step", 2, 1), ("relay", 4), ("mult", 0), ("carry", 1), ("second", 3),
    ("swap", 3), ("step", 2, 2), ("step", 0, 1), ("relay", 3), ("settle", 1), ("swap", 5), ("step", 2, 3),
    ("mult", 6), ("relay", 5), ("carry", 3), ("mult", 1), ("finish", 2), ("last", 2), ("step", 0, 2), ("mult", 4),
    ("step", 6, 1), ("step", 0, 3), ("settle", 3), ("swap", 7), ("relay", 7), ("step", 1, 1), ("mult", 3),
    ("finish", 0), ("step", 4, 1), ("mult", 5), ("last", 0), ("step", 6, 2), ("mult", 7), ("step", 1, 2),
    ("step", 3, 1), ("step", 4, 2), ("step", 6, 3), ("step", 5, 1), ("step", 7, 1), ("step", 1, 3), ("step", 3, 2),
    ("finish", 6), ("step", 4, 3), ("last", 6), ("step", 5, 2), ("step", 7, 2), ("step", 3, 3), ("finish", 1),
    ("last", 1), ("step", 5, 3), ("step", 7, 3), ("finish", 4), ("last", 4), ("finish", 3), ("last", 3),
    ("finish", 5), ("last", 5), ("finish", 7), ("last", 7),
)


def nt(a, b):
    return lax.dot_general(a, b, (((1,), (1,)), ((), ())), preferred_element_type=F32)


def tn(a, b):
    return lax.dot_general(a, b, (((0,), (0,)), ((), ())), preferred_element_type=F32)


def nn(a, b):
    return jnp.dot(a, b, preferred_element_type=F32)


def kernel(
    hid_hbm, q_hbm, k_hbm, v_hbm, fo_hbm, do_hbm, lse, order, lengths, inv,
    gout, wout,
    hid, q, k, v, fo, do,
    kvr, bias, cosf, sinf, delta, dq_acc, home, one_part,
    two_send, two_recv, car_send, car_recv, pri_send, pri_recv,
    g, xt, xt_core, xt_far, gq, part, rs_send, rs_recv, fin, fin_send, fin_recv,
    in_s, kv_s, kv_r, ret_s, ret_r, xt_s, xt_r, gx_s, gx_r, rs_ss, rs_rs, fin_s, fin_r,
):
    z = lax.axis_index("inner")
    oo = lax.axis_index("outer")
    f = lax.axis_index("fsdp")
    n_outer = lax.axis_size("outer")
    xh = f // 2
    c = f % 2
    up = {"inner": (z + 1) % RING}
    down = {"inner": (z + RING - 1) % RING}
    nxt = {"outer": (oo + 1) % n_outer}
    prv = {"outer": (oo + n_outer - 1) % n_outer}
    core = {"fsdp": xh * 2 + 1 - c}
    far = {"fsdp": (1 - xh) * 2 + c}

    sends = []
    cps = {}

    def send(name, src, dst, ss, rs, to):
        cp = pltpu.make_async_remote_copy(
            src_ref=src, dst_ref=dst, send_sem=ss, recv_sem=rs, device_id=to, device_id_type=MESH
        )
        cp.start()
        sends.append(cp)
        cps[name] = cp

    barrier = pltpu.get_barrier_semaphore()
    for to in (up, down, nxt, prv, core, far):
        pl.semaphore_signal(barrier, inc=1, device_id=to, device_id_type=MESH)
    loads = {}
    for i, (name, src, dst) in enumerate((
        ("k", k_hbm, k), ("v", v_hbm, v), ("hid", hid_hbm, hid), ("q", q_hbm, q), ("do", do_hbm, do), ("fo", fo_hbm, fo)
    )):
        loads[name] = pltpu.make_async_copy(src, dst, in_s.at[i])
        loads[name].start()
    loads["k"].wait()
    loads["v"].wait()
    pl.semaphore_wait(barrier, 6)

    def halo(name, slot, gi, srcs, to):
        cols = pl.ds(gi * 256, 256)
        for j in range(2):
            send(
                (name, gi, j), srcs[j].at[:, cols], kvr.at[slot, j, :, cols],
                kv_s.at[slot, gi, j], kv_r.at[slot, gi, j], to,
            )

    def one(gi):
        halo("one", 0, gi, (k, v), up)

    def pri(gi):
        halo("pri", 2, gi, (k, v), nxt)

    def fwd(gi):
        for j in range(2):
            cps["one", gi, j].wait_recv()
        halo("two", 1, gi, (kvr.at[0, 0], kvr.at[0, 1]), up)

    def turn():
        loads["hid"].wait()
        turned = hid[...].T
        for i in range(2 * RING):
            xt[i // 2, i % 2] = turned[i * ROWS : (i + 1) * ROWS]
        send("xc", xt.at[:, xh], xt_core, xt_s.at[0], xt_r.at[0], core)
        send("xf", xt.at[:, 1 - xh], xt_far.at[0], xt_s.at[1], xt_r.at[1], far)

    def xon():
        cps["xf"].wait_recv()
        send("xd", xt_far.at[0], xt_far.at[1], xt_s.at[2], xt_r.at[2], core)

    def xready():
        cps["xc"].wait_recv()
        cps["xd"].wait_recv()

    rows_i = lax.broadcasted_iota(jnp.int32, (TOK, TOK), 0)
    cols_i = lax.broadcasted_iota(jnp.int32, (TOK, TOK), 1)

    def block(outer_pos, inner_pos):
        return order[(outer_pos % n_outer) * RING + inner_pos % RING] * TOK

    def prep():
        starts = [jnp.int32(0)]
        for i in range(3):
            starts.append(starts[-1] + lengths[0, i])

        def doc_of(pos):
            total = jnp.zeros(pos.shape, jnp.int32)
            for s in starts:
                total = total + (pos >= s).astype(jnp.int32)
            return total

        qpos = block(oo, z) + cols_i
        qdoc = doc_of(qpos)
        slots = ((oo, z), (oo, z + RING - 1), (oo, z + RING - 2), (oo + n_outer - 1, z))
        for i, (a, b) in enumerate(slots):
            kpos = block(a, b) + rows_i
            live = (kpos <= qpos) & (doc_of(kpos) == qdoc)
            bias[i] = jnp.where(live, F32(0.0), F32(DEAD))
        angle = (block(oo, z) + rows_i).astype(F32) * inv[0:1, :]
        cosf[...] = jnp.cos(angle)
        sine = jnp.sin(angle)
        sinf[...] = jnp.where(cols_i < HD // 2, sine, -sine)
        for name in ("q", "do", "fo"):
            loads[name].wait()
        ones = jnp.ones((8, HD), BF16)
        for h in range(HQ):
            cols = slice(h * HD, (h + 1) * HD)
            prod = do[:, cols].astype(F32) * fo[:, cols].astype(F32)
            hi = prod.astype(BF16)
            lo = (prod - hi.astype(F32)).astype(BF16)
            delta[h : h + 1] = (nt(ones, hi) + nt(ones, lo))[0:1]

    def unrotate(grad):
        return grad * cosf[...] + pltpu.roll(grad, HD // 2, 1) * sinf[...]

    def attend(h, kk, vv, bb):
        a, b = slice(2 * h * HD, (2 * h + 1) * HD), slice((2 * h + 1) * HD, (2 * h + 2) * HD)
        qs = jnp.concatenate([q[:, a], q[:, b]], axis=0)
        dos = jnp.concatenate([do[:, a], do[:, b]], axis=0)
        lse_h = jnp.concatenate([lse[2 * h : 2 * h + 1], lse[2 * h + 1 : 2 * h + 2]], axis=1)
        delta_h = jnp.concatenate([delta[2 * h : 2 * h + 1], delta[2 * h + 1 : 2 * h + 2]], axis=1)
        capped = jnp.tanh(nt(kk, qs) * F32(1.0 / 600.0))
        prob = jnp.exp(F32(50.0) * capped - lse_h + jnp.concatenate([bb, bb], axis=1))
        dprob = nt(vv, dos)
        ds = (prob * (dprob - delta_h) * (F32(1.0 / 12.0) - F32(1.0 / 12.0) * (capped * capped))).astype(BF16)
        return tn(ds, kk), nn(ds, qs), nn(prob.astype(BF16), dos)

    def first(gi):
        for hh in range(2):
            h = gi * 2 + hh
            cols = slice(h * HD, (h + 1) * HD)
            kk = jnp.concatenate([k[:, cols], kvr[0, 0, :, cols]], axis=0)
            vv = jnp.concatenate([v[:, cols], kvr[0, 1, :, cols]], axis=0)
            dq, dk, dv = attend(h, kk, vv, bias[0:2].reshape(2 * TOK, TOK))
            dq_acc[h] = dq
            for j, val in enumerate((dk, dv)):
                home[gi, hh, j] = val[0:TOK]
                one_part[gi, hh, j] = val[TOK : 2 * TOK]

    def second(gi):
        for j in range(2):
            cps["two", gi, j].wait_recv()
            cps["pri", gi, j].wait_recv()
        for hh in range(2):
            h = gi * 2 + hh
            cols = slice(h * HD, (h + 1) * HD)
            kk = kvr[1:3, 0, :, cols].reshape(2 * TOK, HD)
            vv = kvr[1:3, 1, :, cols].reshape(2 * TOK, HD)
            dq, dk, dv = attend(h, kk, vv, bias[2:4].reshape(2 * TOK, TOK))
            for j, val in enumerate((dk, dv)):
                two_send[gi, hh, j] = val[0:TOK].astype(BF16)
                pri_send[gi, hh, j] = val[TOK : 2 * TOK].astype(BF16)
            total = dq_acc[h] + dq
            for i in range(2):
                at = (2 * h + i) * HD
                g[:, at : at + HD] = unrotate(total[i * TOK : (i + 1) * TOK]).astype(BF16)
        send(("ret", gi), two_send.at[gi], two_recv.at[gi], ret_s.at[1, gi], ret_r.at[1, gi], down)
        send(("rpri", gi), pri_send.at[gi], pri_recv.at[gi], ret_s.at[0, gi], ret_r.at[0, gi], prv)

    def carry(gi):
        cps["ret", gi].wait_recv()
        car_send[gi] = (two_recv[gi].astype(F32) + one_part[gi]).astype(BF16)
        send(("car", gi), car_send.at[gi], car_recv.at[gi], ret_s.at[2, gi], ret_r.at[2, gi], down)

    def settle(gi):
        cps["car", gi].wait_recv()
        cps["rpri", gi].wait_recv()
        for hh in range(2):
            h = gi * 2 + hh
            dk, dv = [
                home[gi, hh, j] + car_recv[gi, hh, j].astype(F32) + pri_recv[gi, hh, j].astype(F32)
                for j in range(2)
            ]
            at = HQ * HD + h * HD
            g[:, at : at + HD] = unrotate(dk).astype(BF16)
            at = (HQ + HK) * HD + h * HD
            g[:, at : at + HD] = dv.astype(BF16)

    def base(ch, who):
        lo, hi = CHUNKS[ch]
        return pl.ds(pl.multiple_of(lo + who * (hi - lo), HALF), HALF)

    def swap(ch):
        gq[ch, 0] = g[:, base(ch, c)]
        send(("g1", ch), g.at[:, base(ch, 1 - c)], gq.at[ch, 1], gx_s.at[ch, 0], gx_r.at[ch, 0], core)
        send(("g2", ch), gq.at[ch, 0], gq.at[ch, 2], gx_s.at[ch, 1], gx_r.at[ch, 1], far)

    def relay(ch):
        cps["g1", ch].wait_recv()
        send(("g3", ch), gq.at[ch, 1], gq.at[ch, 3], gx_s.at[ch, 2], gx_r.at[ch, 2], far)

    def term(ch, chain, s):
        way, hops = CHAINS[ch][chain]
        return part[ch, (z + 2 * RING + way * (hops - s)) % RING]

    def hop(ch, chain, s, val):
        rs_send[ch, chain, s] = val.astype(BF16)
        send(
            ("rs", ch, chain, s), rs_send.at[ch, chain, s], rs_recv.at[ch, chain, s],
            rs_ss.at[ch, chain, s], rs_rs.at[ch, chain, s], up if CHAINS[ch][chain][0] > 0 else down,
        )

    def mult(ch):
        cps["g2", ch].wait_recv()
        cps["g3", ch].wait_recv()
        gs = gq[ch].reshape(QUAD * TOK, HALF)
        for piece in range(2):
            at = slice(piece * 4, piece * 4 + 4)
            xs = jnp.concatenate(
                [xt.at[:, xh][at], xt_core[at], xt_far[0, at], xt_far[1, at]], axis=-1
            ).reshape(4 * ROWS, QUAD * TOK)
            part[ch, at] = nn(xs, gs).reshape(4, ROWS, HALF)
        for chain in range(2):
            hop(ch, chain, 0, term(ch, chain, 0))

    def step(ch, s):
        for chain in range(2):
            if s < CHAINS[ch][chain][1]:
                cps["rs", ch, chain, s - 1].wait_recv()
                hop(ch, chain, s, rs_recv[ch, chain, s - 1].astype(F32) + term(ch, chain, s))

    def finish(ch):
        val = part[ch, z]
        for chain in range(2):
            end = CHAINS[ch][chain][1] - 1
            cps["rs", ch, chain, end].wait_recv()
            val = val + rs_recv[ch, chain, end].astype(F32)
        fin[ch, 0] = val[0 : ROWS // 2]
        fin[ch, 1] = val[ROWS // 2 :]
        fin_send[ch] = fin[ch, 1 - c].astype(BF16)
        send(("fin", ch), fin_send.at[ch], fin_recv.at[ch], fin_s.at[ch], fin_r.at[ch], core)
        wout[:, base(ch, c)] = fin[ch, c].astype(BF16)

    def last(ch):
        cps["fin", ch].wait_recv()
        wout[:, base(ch, 1 - c)] = fin_recv[ch]

    steps = {
        "one": one, "pri": pri, "fwd": fwd, "turn": turn, "prep": prep, "xon": xon, "xready": xready,
        "first": first, "second": second, "carry": carry, "settle": settle, "swap": swap, "relay": relay,
        "mult": mult, "step": step, "finish": finish, "last": last,
    }
    settled = 0
    for name, *which in ORDER:
        steps[name](*which)
        if name in ("second", "settle"):
            settled += 1
            if settled == 2 * GROUPS:
                store = pltpu.make_async_copy(g, gout, in_s.at[6])
                store.start()
    store.wait()
    for cp in sends:
        cp.wait_send()


def local(hidden_in, queries, keys, values, fwd_out, out_grad, lse, block_order, doc_lengths):
    freq = 10000.0 ** (-2.0 * np.arange(HD // 2, dtype=np.float32) / HD)
    inv = jnp.asarray(np.broadcast_to(np.concatenate([freq, freq])[None, :], (8, HD)).astype(np.float32))
    vm = pl.BlockSpec(memory_space=pltpu.VMEM)
    sm = pl.BlockSpec(memory_space=pltpu.SMEM)
    hbm = pl.BlockSpec(memory_space=pl.ANY)
    ret = pltpu.VMEM((GROUPS, 2, 2, TOK, HD), BF16)
    dma = pltpu.SemaphoreType.DMA
    nch = len(CHUNKS)
    qkv, weights = pl.pallas_call(
        kernel,
        out_shape=(
            jax.ShapeDtypeStruct((TOK, COLS), BF16),
            jax.ShapeDtypeStruct((ROWS // 2, COLS), BF16),
        ),
        in_specs=[hbm] * 6 + [vm, sm, sm, vm],
        out_specs=(hbm, vm),
        scratch_shapes=[
            pltpu.VMEM((TOK, D), BF16),
            pltpu.VMEM((TOK, HQ * HD), BF16),
            pltpu.VMEM((TOK, HK * HD), BF16),
            pltpu.VMEM((TOK, HK * HD), BF16),
            pltpu.VMEM((TOK, HQ * HD), BF16),
            pltpu.VMEM((TOK, HQ * HD), BF16),
            pltpu.VMEM((3, 2, TOK, HK * HD), BF16),
            pltpu.VMEM((4, TOK, TOK), F32),
            pltpu.VMEM((TOK, HD), F32),
            pltpu.VMEM((TOK, HD), F32),
            pltpu.VMEM((HQ, TOK), F32),
            pltpu.VMEM((HK, 2 * TOK, HD), F32),
            pltpu.VMEM((GROUPS, 2, 2, TOK, HD), F32),
            pltpu.VMEM((GROUPS, 2, 2, TOK, HD), F32),
            ret, ret, ret, ret, ret, ret,
            pltpu.VMEM((TOK, COLS), BF16),
            pltpu.VMEM((RING, 2, ROWS, TOK), BF16),
            pltpu.VMEM((RING, ROWS, TOK), BF16),
            pltpu.VMEM((2, RING, ROWS, TOK), BF16),
            pltpu.VMEM((nch, QUAD, TOK, HALF), BF16),
            pltpu.VMEM((nch, RING, ROWS, HALF), F32),
            pltpu.VMEM((nch, 2, 4, ROWS, HALF), BF16),
            pltpu.VMEM((nch, 2, 4, ROWS, HALF), BF16),
            pltpu.VMEM((nch, 2, ROWS // 2, HALF), F32),
            pltpu.VMEM((nch, ROWS // 2, HALF), BF16),
            pltpu.VMEM((nch, ROWS // 2, HALF), BF16),
            dma((7,)),
            dma((3, GROUPS, 2)), dma((3, GROUPS, 2)),
            dma((3, GROUPS)), dma((3, GROUPS)),
            dma((3,)), dma((3,)),
            dma((nch, 3)), dma((nch, 3)),
            dma((nch, 2, 4)), dma((nch, 2, 4)),
            dma((nch,)), dma((nch,)),
        ],
        compiler_params=pltpu.CompilerParams(
            collective_id=0, has_side_effects=True, vmem_limit_bytes=58 * 1024 * 1024
        ),
        cost_estimate=pl.CostEstimate(flops=4 * 10**9, bytes_accessed=6 * 10**6, transcendentals=2 * 10**6),
    )(
        hidden_in[0], queries[0], keys[0], values[0], fwd_out[0], out_grad[0], lse[0],
        block_order, doc_lengths, inv,
    )
    return (qkv[None], weights[None])


def solution(mesh):
    tokens = P("fsdp", ("outer", "inner"), None)
    in_specs = (tokens,) * 6 + (P("fsdp", None, ("outer", "inner")), P(), P("fsdp", None))
    out_specs = (tokens, P("outer", ("inner", "fsdp"), None))
    return jax.shard_map(local, mesh=mesh, in_specs=in_specs, out_specs=out_specs, check_vma=False)
```

```python
import functools

import jax
import jax.numpy as jnp
import numpy as np
from jax import lax
from jax.experimental import pallas as pl
from jax.experimental.pallas import tpu as pltpu
from jax.sharding import PartitionSpec as P

MESH = pl.DeviceIdType.MESH
F32 = jnp.float32
BF16 = jnp.bfloat16

HQ = 16
HK = 8
HD = 128
TOK = 128
D = 2304
COLS = 4096
RING = 8
QUAD = 4
GROUPS = 4
ROWS = D // RING // 2
HALF = 256
DEAD = -1e30

CHUNKS = tuple((512 * i, 512 * i + 256) for i in range(4)) + tuple(
    (2048 + 256 * i, 3072 + 256 * i) for i in range(4)
)
LONG_UP = ((1, 4), (-1, 3))
LONG_DOWN = ((1, 3), (-1, 4))
CHAINS = (LONG_UP, LONG_UP, LONG_UP, LONG_DOWN, LONG_UP, LONG_DOWN, LONG_UP, LONG_DOWN)
ORDER = (
    ("pri", 0), ("pri", 2), ("one", 2), ("turn",), ("prep",), ("one", 0), ("fwd", 2), ("first", 2), ("fwd", 0),
    ("first", 0), ("second", 2), ("swap", 2), ("relay", 2), ("one", 1), ("pri", 1), ("second", 0), ("swap", 0),
    ("xon",), ("relay", 0), ("carry", 2), ("xready",), ("fwd", 1), ("first", 1), ("one", 3), ("carry", 0), ("pri", 3),
    ("mult", 2), ("settle", 2), ("swap", 6), ("second", 1), ("relay", 6), ("swap", 1), ("relay", 1), ("fwd", 3),
    ("first", 3), ("settle", 0), ("swap", 4), ("step", 2, 1), ("relay", 4), ("mult", 0), ("carry", 1), ("second", 3),
    ("swap", 3), ("step", 2, 2), ("step", 0, 1), ("relay", 3), ("settle", 1), ("swap", 5), ("step", 2, 3),
    ("mult", 6), ("relay", 5), ("carry", 3), ("mult", 1), ("finish", 2), ("last", 2), ("step", 0, 2), ("mult", 4),
    ("step", 6, 1), ("step", 0, 3), ("settle", 3), ("swap", 7), ("relay", 7), ("step", 1, 1), ("mult", 3),
    ("finish", 0), ("step", 4, 1), ("mult", 5), ("last", 0), ("step", 6, 2), ("mult", 7), ("step", 1, 2),
    ("step", 3, 1), ("step", 4, 2), ("step", 6, 3), ("step", 5, 1), ("step", 7, 1), ("step", 1, 3), ("step", 3, 2),
    ("finish", 6), ("step", 4, 3), ("last", 6), ("step", 5, 2), ("step", 7, 2), ("step", 3, 3), ("finish", 1),
    ("last", 1), ("step", 5, 3), ("step", 7, 3), ("finish", 4), ("last", 4), ("finish", 3), ("last", 3),
    ("finish", 5), ("last", 5), ("finish", 7), ("last", 7),
)


def nt(a, b):
    return lax.dot_general(a, b, (((1,), (1,)), ((), ())), preferred_element_type=F32)


def tn(a, b):
    return lax.dot_general(a, b, (((0,), (0,)), ((), ())), preferred_element_type=F32)


def nn(a, b):
    return jnp.dot(a, b, preferred_element_type=F32)


def kernel(
    hid_hbm, q_hbm, k_hbm, v_hbm, fo_hbm, do_hbm, lse_hbm, order_hbm, lengths_hbm, inv_hbm,
    gout, wout,
    hid, q, k, v, fo, do, lse, inv, order, lengths,
    kvr, bias, cosf, sinf, delta, dq_acc, home, one_part,
    two_send, two_recv, car_send, car_recv, pri_send, pri_recv,
    g, xt, xt_core, xt_far, gq, part, rs_send, rs_recv, fin, fin_send, fin_recv,
    in_s, kv_s, kv_r, ret_s, ret_r, xt_s, xt_r, gx_s, gx_r, rs_ss, rs_rs, fin_s, fin_r,
):
    z = lax.axis_index("inner")
    oo = lax.axis_index("outer")
    f = lax.axis_index("fsdp")
    n_outer = lax.axis_size("outer")
    xh = f // 2
    c = f % 2
    up = {"inner": (z + 1) % RING}
    down = {"inner": (z + RING - 1) % RING}
    nxt = {"outer": (oo + 1) % n_outer}
    prv = {"outer": (oo + n_outer - 1) % n_outer}
    core = {"fsdp": xh * 2 + 1 - c}
    far = {"fsdp": (1 - xh) * 2 + c}

    sends = []
    cps = {}

    def send(name, src, dst, ss, rs, to):
        cp = pltpu.make_async_remote_copy(
            src_ref=src, dst_ref=dst, send_sem=ss, recv_sem=rs, device_id=to, device_id_type=MESH
        )
        cp.start()
        sends.append(cp)
        cps[name] = cp

    barrier = pltpu.get_barrier_semaphore()
    for to in (up, down, nxt, prv, core, far):
        pl.semaphore_signal(barrier, inc=1, device_id=to, device_id_type=MESH)
    loads = {}
    for i, (name, src, dst) in enumerate((
        ("k", k_hbm, k), ("v", v_hbm, v), ("hid", hid_hbm, hid), ("q", q_hbm, q), ("do", do_hbm, do), ("fo", fo_hbm, fo),
        ("lse", lse_hbm, lse), ("inv", inv_hbm, inv),
        ("order", order_hbm, order), ("lengths", lengths_hbm, lengths),
    )):
        loads[name] = pltpu.make_async_copy(src, dst, in_s.at[i])
        loads[name].start()
    loads["k"].wait()
    loads["v"].wait()
    pl.semaphore_wait(barrier, 6)

    def halo(name, slot, gi, srcs, to):
        cols = pl.ds(gi * 256, 256)
        for j in range(2):
            send(
                (name, gi, j), srcs[j].at[:, cols], kvr.at[slot, j, :, cols],
                kv_s.at[slot, gi, j], kv_r.at[slot, gi, j], to,
            )

    def one(gi):
        halo("one", 0, gi, (k, v), up)

    def pri(gi):
        halo("pri", 2, gi, (k, v), nxt)

    def fwd(gi):
        for j in range(2):
            cps["one", gi, j].wait_recv()
        halo("two", 1, gi, (kvr.at[0, 0], kvr.at[0, 1]), up)

    def turn():
        loads["hid"].wait()
        turned = hid[...].T
        for i in range(2 * RING):
            xt[i // 2, i % 2] = turned[i * ROWS : (i + 1) * ROWS]
        send("xc", xt.at[:, xh], xt_core, xt_s.at[0], xt_r.at[0], core)
        send("xf", xt.at[:, 1 - xh], xt_far.at[0], xt_s.at[1], xt_r.at[1], far)

    def xon():
        cps["xf"].wait_recv()
        send("xd", xt_far.at[0], xt_far.at[1], xt_s.at[2], xt_r.at[2], core)

    def xready():
        cps["xc"].wait_recv()
        cps["xd"].wait_recv()

    rows_i = lax.broadcasted_iota(jnp.int32, (TOK, TOK), 0)
    cols_i = lax.broadcasted_iota(jnp.int32, (TOK, TOK), 1)

    def block(outer_pos, inner_pos):
        return order[(outer_pos % n_outer) * RING + inner_pos % RING] * TOK

    def prep():
        loads["order"].wait()
        loads["lengths"].wait()
        starts = [jnp.int32(0)]
        for i in range(3):
            starts.append(starts[-1] + lengths[0, i])

        def doc_of(pos):
            total = jnp.zeros(pos.shape, jnp.int32)
            for s in starts:
                total = total + (pos >= s).astype(jnp.int32)
            return total

        qpos = block(oo, z) + cols_i
        qdoc = doc_of(qpos)
        slots = ((oo, z), (oo, z + RING - 1), (oo, z + RING - 2), (oo + n_outer - 1, z))
        for i, (a, b) in enumerate(slots):
            kpos = block(a, b) + rows_i
            live = (kpos <= qpos) & (doc_of(kpos) == qdoc)
            bias[i] = jnp.where(live, F32(0.0), F32(DEAD))
        loads["inv"].wait()
        loads["lse"].wait()
        angle = (block(oo, z) + rows_i).astype(F32) * inv[0:1, :]
        cosf[...] = jnp.cos(angle)
        sine = jnp.sin(angle)
        sinf[...] = jnp.where(cols_i < HD // 2, sine, -sine)
        for name in ("q", "do", "fo"):
            loads[name].wait()
        ones = jnp.ones((8, HD), BF16)
        for h in range(HQ):
            cols = slice(h * HD, (h + 1) * HD)
            prod = do[:, cols].astype(F32) * fo[:, cols].astype(F32)
            hi = prod.astype(BF16)
            lo = (prod - hi.astype(F32)).astype(BF16)
            delta[h : h + 1] = (nt(ones, hi) + nt(ones, lo))[0:1]

    def unrotate(grad):
        return grad * cosf[...] + pltpu.roll(grad, HD // 2, 1) * sinf[...]

    def attend(h, kk, vv, bb):
        a, b = slice(2 * h * HD, (2 * h + 1) * HD), slice((2 * h + 1) * HD, (2 * h + 2) * HD)
        qs = jnp.concatenate([q[:, a], q[:, b]], axis=0)
        dos = jnp.concatenate([do[:, a], do[:, b]], axis=0)
        lse_h = jnp.concatenate([lse[2 * h : 2 * h + 1], lse[2 * h + 1 : 2 * h + 2]], axis=1)
        delta_h = jnp.concatenate([delta[2 * h : 2 * h + 1], delta[2 * h + 1 : 2 * h + 2]], axis=1)
        capped = jnp.tanh(nt(kk, qs) * F32(1.0 / 600.0))
        prob = jnp.exp(F32(50.0) * capped - lse_h + jnp.concatenate([bb, bb], axis=1))
        dprob = nt(vv, dos)
        ds = (prob * (dprob - delta_h) * (F32(1.0 / 12.0) - F32(1.0 / 12.0) * (capped * capped))).astype(BF16)
        return tn(ds, kk), nn(ds, qs), nn(prob.astype(BF16), dos)

    def first(gi):
        for hh in range(2):
            h = gi * 2 + hh
            cols = slice(h * HD, (h + 1) * HD)
            kk = jnp.concatenate([k[:, cols], kvr[0, 0, :, cols]], axis=0)
            vv = jnp.concatenate([v[:, cols], kvr[0, 1, :, cols]], axis=0)
            dq, dk, dv = attend(h, kk, vv, bias[0:2].reshape(2 * TOK, TOK))
            dq_acc[h] = dq
            for j, val in enumerate((dk, dv)):
                home[gi, hh, j] = val[0:TOK]
                one_part[gi, hh, j] = val[TOK : 2 * TOK]

    def second(gi):
        for j in range(2):
            cps["two", gi, j].wait_recv()
            cps["pri", gi, j].wait_recv()
        for hh in range(2):
            h = gi * 2 + hh
            cols = slice(h * HD, (h + 1) * HD)
            kk = kvr[1:3, 0, :, cols].reshape(2 * TOK, HD)
            vv = kvr[1:3, 1, :, cols].reshape(2 * TOK, HD)
            dq, dk, dv = attend(h, kk, vv, bias[2:4].reshape(2 * TOK, TOK))
            for j, val in enumerate((dk, dv)):
                two_send[gi, hh, j] = val[0:TOK].astype(BF16)
                pri_send[gi, hh, j] = val[TOK : 2 * TOK].astype(BF16)
            total = dq_acc[h] + dq
            for i in range(2):
                at = (2 * h + i) * HD
                g[:, at : at + HD] = unrotate(total[i * TOK : (i + 1) * TOK]).astype(BF16)
        send(("ret", gi), two_send.at[gi], two_recv.at[gi], ret_s.at[1, gi], ret_r.at[1, gi], down)
        send(("rpri", gi), pri_send.at[gi], pri_recv.at[gi], ret_s.at[0, gi], ret_r.at[0, gi], prv)

    def carry(gi):
        cps["ret", gi].wait_recv()
        car_send[gi] = (two_recv[gi].astype(F32) + one_part[gi]).astype(BF16)
        send(("car", gi), car_send.at[gi], car_recv.at[gi], ret_s.at[2, gi], ret_r.at[2, gi], down)

    def settle(gi):
        cps["car", gi].wait_recv()
        cps["rpri", gi].wait_recv()
        for hh in range(2):
            h = gi * 2 + hh
            dk, dv = [
                home[gi, hh, j] + car_recv[gi, hh, j].astype(F32) + pri_recv[gi, hh, j].astype(F32)
                for j in range(2)
            ]
            at = HQ * HD + h * HD
            g[:, at : at + HD] = unrotate(dk).astype(BF16)
            at = (HQ + HK) * HD + h * HD
            g[:, at : at + HD] = dv.astype(BF16)

    def base(ch, who):
        lo, hi = CHUNKS[ch]
        return pl.ds(pl.multiple_of(lo + who * (hi - lo), HALF), HALF)

    def swap(ch):
        gq[ch, 0] = g[:, base(ch, c)]
        send(("g1", ch), g.at[:, base(ch, 1 - c)], gq.at[ch, 1], gx_s.at[ch, 0], gx_r.at[ch, 0], core)
        send(("g2", ch), gq.at[ch, 0], gq.at[ch, 2], gx_s.at[ch, 1], gx_r.at[ch, 1], far)

    def relay(ch):
        cps["g1", ch].wait_recv()
        send(("g3", ch), gq.at[ch, 1], gq.at[ch, 3], gx_s.at[ch, 2], gx_r.at[ch, 2], far)

    def term(ch, chain, s):
        way, hops = CHAINS[ch][chain]
        return part[ch, (z + 2 * RING + way * (hops - s)) % RING]

    def hop(ch, chain, s, val):
        rs_send[ch, chain, s] = val.astype(BF16)
        send(
            ("rs", ch, chain, s), rs_send.at[ch, chain, s], rs_recv.at[ch, chain, s],
            rs_ss.at[ch, chain, s], rs_rs.at[ch, chain, s], up if CHAINS[ch][chain][0] > 0 else down,
        )

    def mult(ch):
        cps["g2", ch].wait_recv()
        cps["g3", ch].wait_recv()
        gs = gq[ch].reshape(QUAD * TOK, HALF)
        for piece in range(2):
            at = slice(piece * 4, piece * 4 + 4)
            xs = jnp.concatenate(
                [xt.at[:, xh][at], xt_core[at], xt_far[0, at], xt_far[1, at]], axis=-1
            ).reshape(4 * ROWS, QUAD * TOK)
            part[ch, at] = nn(xs, gs).reshape(4, ROWS, HALF)
        for chain in range(2):
            hop(ch, chain, 0, term(ch, chain, 0))

    def step(ch, s):
        for chain in range(2):
            if s < CHAINS[ch][chain][1]:
                cps["rs", ch, chain, s - 1].wait_recv()
                hop(ch, chain, s, rs_recv[ch, chain, s - 1].astype(F32) + term(ch, chain, s))

    def finish(ch):
        val = part[ch, z]
        for chain in range(2):
            end = CHAINS[ch][chain][1] - 1
            cps["rs", ch, chain, end].wait_recv()
            val = val + rs_recv[ch, chain, end].astype(F32)
        fin[ch, 0] = val[0 : ROWS // 2]
        fin[ch, 1] = val[ROWS // 2 :]
        fin_send[ch] = fin[ch, 1 - c].astype(BF16)
        send(("fin", ch), fin_send.at[ch], fin_recv.at[ch], fin_s.at[ch], fin_r.at[ch], core)
        wout[:, base(ch, c)] = fin[ch, c].astype(BF16)

    def last(ch):
        cps["fin", ch].wait_recv()
        wout[:, base(ch, 1 - c)] = fin_recv[ch]

    steps = {
        "one": one, "pri": pri, "fwd": fwd, "turn": turn, "prep": prep, "xon": xon, "xready": xready,
        "first": first, "second": second, "carry": carry, "settle": settle, "swap": swap, "relay": relay,
        "mult": mult, "step": step, "finish": finish, "last": last,
    }
    settled = 0
    for name, *which in ORDER:
        steps[name](*which)
        if name in ("second", "settle"):
            settled += 1
            if settled == 2 * GROUPS:
                store = pltpu.make_async_copy(g, gout, in_s.at[10])
                store.start()
    store.wait()
    for cp in sends:
        cp.wait_send()


def hand_over(qkv, weights, qkv_out, weights_out):
    qkv_out[...] = qkv[...]
    weights_out[...] = weights[...]


def local(hidden_in, queries, keys, values, fwd_out, out_grad, lse, block_order, doc_lengths):
    freq = 10000.0 ** (-2.0 * np.arange(HD // 2, dtype=np.float32) / HD)
    inv = jnp.asarray(np.broadcast_to(np.concatenate([freq, freq])[None, :], (8, HD)).astype(np.float32))
    vm = pl.BlockSpec(memory_space=pltpu.VMEM)
    sm = pl.BlockSpec(memory_space=pltpu.SMEM)
    hbm = pl.BlockSpec(memory_space=pl.ANY)
    ret = pltpu.VMEM((GROUPS, 2, 2, TOK, HD), BF16)
    dma = pltpu.SemaphoreType.DMA
    nch = len(CHUNKS)
    qkv, weights = pl.pallas_call(
        kernel,
        out_shape=(
            jax.ShapeDtypeStruct((TOK, COLS), BF16),
            jax.ShapeDtypeStruct((ROWS // 2, COLS), BF16),
        ),
        in_specs=[hbm] * 10,
        out_specs=(hbm, vm),
        scratch_shapes=[
            pltpu.VMEM((TOK, D), BF16),
            pltpu.VMEM((TOK, HQ * HD), BF16),
            pltpu.VMEM((TOK, HK * HD), BF16),
            pltpu.VMEM((TOK, HK * HD), BF16),
            pltpu.VMEM((TOK, HQ * HD), BF16),
            pltpu.VMEM((TOK, HQ * HD), BF16),
            pltpu.VMEM((HQ, TOK), F32),
            pltpu.VMEM((8, HD), F32),
            pltpu.SMEM((64,), jnp.int32),
            pltpu.SMEM((1, 4), jnp.int32),
            pltpu.VMEM((3, 2, TOK, HK * HD), BF16),
            pltpu.VMEM((4, TOK, TOK), F32),
            pltpu.VMEM((TOK, HD), F32),
            pltpu.VMEM((TOK, HD), F32),
            pltpu.VMEM((HQ, TOK), F32),
            pltpu.VMEM((HK, 2 * TOK, HD), F32),
            pltpu.VMEM((GROUPS, 2, 2, TOK, HD), F32),
            pltpu.VMEM((GROUPS, 2, 2, TOK, HD), F32),
            ret, ret, ret, ret, ret, ret,
            pltpu.VMEM((TOK, COLS), BF16),
            pltpu.VMEM((RING, 2, ROWS, TOK), BF16),
            pltpu.VMEM((RING, ROWS, TOK), BF16),
            pltpu.VMEM((2, RING, ROWS, TOK), BF16),
            pltpu.VMEM((nch, QUAD, TOK, HALF), BF16),
            pltpu.VMEM((nch, RING, ROWS, HALF), F32),
            pltpu.VMEM((nch, 2, 4, ROWS, HALF), BF16),
            pltpu.VMEM((nch, 2, 4, ROWS, HALF), BF16),
            pltpu.VMEM((nch, 2, ROWS // 2, HALF), F32),
            pltpu.VMEM((nch, ROWS // 2, HALF), BF16),
            pltpu.VMEM((nch, ROWS // 2, HALF), BF16),
            dma((11,)),
            dma((3, GROUPS, 2)), dma((3, GROUPS, 2)),
            dma((3, GROUPS)), dma((3, GROUPS)),
            dma((3,)), dma((3,)),
            dma((nch, 3)), dma((nch, 3)),
            dma((nch, 2, 4)), dma((nch, 2, 4)),
            dma((nch,)), dma((nch,)),
        ],
        compiler_params=pltpu.CompilerParams(
            collective_id=0, has_side_effects=True, vmem_limit_bytes=58 * 1024 * 1024
        ),
        cost_estimate=pl.CostEstimate(flops=4 * 10**9, bytes_accessed=6 * 10**6, transcendentals=2 * 10**6),
    )(
        hidden_in[0], queries[0], keys[0], values[0], fwd_out[0], out_grad[0], lse[0],
        block_order, doc_lengths, inv,
    )
    pieces = 2
    blocks = [pl.BlockSpec((TOK, COLS // pieces), lambda i: (0, i)), pl.BlockSpec((ROWS // 2, COLS // pieces), lambda i: (0, i))]
    qkv, weights = pl.pallas_call(
        hand_over,
        out_shape=(
            jax.ShapeDtypeStruct((TOK, COLS), BF16),
            jax.ShapeDtypeStruct((ROWS // 2, COLS), BF16),
        ),
        grid=(pieces,),
        in_specs=blocks,
        out_specs=blocks,
    )(qkv, weights)
    return (qkv[None], weights[None])


def solution(mesh):
    tokens = P("fsdp", ("outer", "inner"), None)
    in_specs = (tokens,) * 6 + (P("fsdp", None, ("outer", "inner")), P(), P("fsdp", None))
    out_specs = (tokens, P("outer", ("inner", "fsdp"), None))
    return jax.shard_map(local, mesh=mesh, in_specs=in_specs, out_specs=out_specs, check_vma=False)
```

```python
import functools

import jax
import jax.numpy as jnp
import numpy as np
from jax import lax
from jax.experimental import pallas as pl
from jax.experimental.pallas import tpu as pltpu
from jax.sharding import PartitionSpec as P

MESH = pl.DeviceIdType.MESH
F32 = jnp.float32
BF16 = jnp.bfloat16

HQ = 16
HK = 8
HD = 128
TOK = 128
D = 2304
COLS = 4096
RING = 8
QUAD = 4
GROUPS = 4
ROWS = D // RING // 2
HALF = 256
DEAD = -1e30

CHUNKS = tuple((512 * i, 512 * i + 256) for i in range(4)) + tuple(
    (2048 + 256 * i, 3072 + 256 * i) for i in range(4)
)
LONG_UP = ((1, 4), (-1, 3))
LONG_DOWN = ((1, 3), (-1, 4))
CHAINS = (LONG_UP, LONG_UP, LONG_UP, LONG_DOWN, LONG_UP, LONG_DOWN, LONG_UP, LONG_DOWN)
ORDER = (
    ("pri", 0), ("pri", 2), ("one", 2), ("turn",), ("prep",), ("one", 0), ("fwd", 2), ("first", 2), ("fwd", 0),
    ("first", 0), ("second", 2), ("swap", 2), ("relay", 2), ("one", 1), ("pri", 1), ("second", 0), ("swap", 0),
    ("xon",), ("relay", 0), ("carry", 2), ("xready",), ("fwd", 1), ("first", 1), ("one", 3), ("carry", 0), ("pri", 3),
    ("mult", 2), ("settle", 2), ("swap", 6), ("second", 1), ("relay", 6), ("swap", 1), ("relay", 1), ("fwd", 3),
    ("first", 3), ("settle", 0), ("swap", 4), ("step", 2, 1), ("relay", 4), ("mult", 0), ("carry", 1), ("second", 3),
    ("swap", 3), ("step", 2, 2), ("step", 0, 1), ("relay", 3), ("settle", 1), ("swap", 5), ("step", 2, 3),
    ("mult", 6), ("relay", 5), ("carry", 3), ("mult", 1), ("finish", 2), ("last", 2), ("step", 0, 2), ("mult", 4),
    ("step", 6, 1), ("step", 0, 3), ("settle", 3), ("swap", 7), ("relay", 7), ("step", 1, 1), ("mult", 3),
    ("finish", 0), ("step", 4, 1), ("mult", 5), ("last", 0), ("step", 6, 2), ("mult", 7), ("step", 1, 2),
    ("step", 3, 1), ("step", 4, 2), ("step", 6, 3), ("step", 5, 1), ("step", 7, 1), ("step", 1, 3), ("step", 3, 2),
    ("finish", 6), ("step", 4, 3), ("last", 6), ("step", 5, 2), ("step", 7, 2), ("step", 3, 3), ("finish", 1),
    ("last", 1), ("step", 5, 3), ("step", 7, 3), ("finish", 4), ("last", 4), ("finish", 3), ("last", 3),
    ("finish", 5), ("last", 5), ("finish", 7), ("last", 7),
)


def nt(a, b):
    return lax.dot_general(a, b, (((1,), (1,)), ((), ())), preferred_element_type=F32)


def tn(a, b):
    return lax.dot_general(a, b, (((0,), (0,)), ((), ())), preferred_element_type=F32)


def nn(a, b):
    return jnp.dot(a, b, preferred_element_type=F32)


def kernel(
    hid_hbm, q_hbm, k_hbm, v_hbm, fo_hbm, do_hbm, lse_hbm, order_hbm, lengths_hbm, inv_hbm,
    gout, wout,
    hid, q, k, v, fo, do, lse, inv, order, lengths,
    kvr, bias, cosf, sinf, delta, dq_acc, home, one_part,
    two_send, two_recv, car_send, car_recv, pri_send, pri_recv,
    g, xt, xt_core, xt_far, gq, part, rs_send, rs_recv, fin, fin_send, fin_recv,
    in_s, kv_s, kv_r, ret_s, ret_r, xt_s, xt_r, gx_s, gx_r, rs_ss, rs_rs, fin_s, fin_r,
):
    z = lax.axis_index("inner")
    oo = lax.axis_index("outer")
    f = lax.axis_index("fsdp")
    n_outer = lax.axis_size("outer")
    xh = f // 2
    c = f % 2
    up = {"inner": (z + 1) % RING}
    down = {"inner": (z + RING - 1) % RING}
    nxt = {"outer": (oo + 1) % n_outer}
    prv = {"outer": (oo + n_outer - 1) % n_outer}
    core = {"fsdp": xh * 2 + 1 - c}
    far = {"fsdp": (1 - xh) * 2 + c}

    sends = []
    cps = {}

    def send(name, src, dst, ss, rs, to):
        cp = pltpu.make_async_remote_copy(
            src_ref=src, dst_ref=dst, send_sem=ss, recv_sem=rs, device_id=to, device_id_type=MESH
        )
        cp.start()
        sends.append(cp)
        cps[name] = cp

    barrier = pltpu.get_barrier_semaphore()
    for to in (up, down, nxt, prv, core, far):
        pl.semaphore_signal(barrier, inc=1, device_id=to, device_id_type=MESH)
    loads = {}
    for i, (name, src, dst) in enumerate((
        ("k", k_hbm, k), ("v", v_hbm, v), ("hid", hid_hbm, hid), ("q", q_hbm, q), ("do", do_hbm, do), ("fo", fo_hbm, fo),
        ("lse", lse_hbm, lse), ("inv", inv_hbm, inv),
        ("order", order_hbm, order), ("lengths", lengths_hbm, lengths),
    )):
        loads[name] = pltpu.make_async_copy(src, dst, in_s.at[i])
        loads[name].start()
    loads["k"].wait()
    loads["v"].wait()
    pl.semaphore_wait(barrier, 6)

    def halo(name, slot, gi, srcs, to):
        cols = pl.ds(gi * 256, 256)
        for j in range(2):
            send(
                (name, gi, j), srcs[j].at[:, cols], kvr.at[slot, j, :, cols],
                kv_s.at[slot, gi, j], kv_r.at[slot, gi, j], to,
            )

    def one(gi):
        halo("one", 0, gi, (k, v), up)

    def pri(gi):
        halo("pri", 2, gi, (k, v), nxt)

    def fwd(gi):
        for j in range(2):
            cps["one", gi, j].wait_recv()
        halo("two", 1, gi, (kvr.at[0, 0], kvr.at[0, 1]), up)

    def turn():
        loads["hid"].wait()
        turned = hid[...].T
        for i in range(2 * RING):
            xt[i // 2, i % 2] = turned[i * ROWS : (i + 1) * ROWS]
        send("xc", xt.at[:, xh], xt_core, xt_s.at[0], xt_r.at[0], core)
        send("xf", xt.at[:, 1 - xh], xt_far.at[0], xt_s.at[1], xt_r.at[1], far)

    def xon():
        cps["xf"].wait_recv()
        send("xd", xt_far.at[0], xt_far.at[1], xt_s.at[2], xt_r.at[2], core)

    def xready():
        cps["xc"].wait_recv()
        cps["xd"].wait_recv()

    rows_i = lax.broadcasted_iota(jnp.int32, (TOK, TOK), 0)
    cols_i = lax.broadcasted_iota(jnp.int32, (TOK, TOK), 1)

    def block(outer_pos, inner_pos):
        return order[(outer_pos % n_outer) * RING + inner_pos % RING] * TOK

    def prep():
        loads["order"].wait()
        loads["lengths"].wait()
        starts = [jnp.int32(0)]
        for i in range(3):
            starts.append(starts[-1] + lengths[0, i])

        def doc_of(pos):
            total = jnp.zeros(pos.shape, jnp.int32)
            for s in starts:
                total = total + (pos >= s).astype(jnp.int32)
            return total

        qpos = block(oo, z) + cols_i
        qdoc = doc_of(qpos)
        slots = ((oo, z), (oo, z + RING - 1), (oo, z + RING - 2), (oo + n_outer - 1, z))
        for i, (a, b) in enumerate(slots):
            kpos = block(a, b) + rows_i
            live = (kpos <= qpos) & (doc_of(kpos) == qdoc)
            bias[i] = jnp.where(live, F32(0.0), F32(DEAD))
        loads["inv"].wait()
        loads["lse"].wait()
        angle = (block(oo, z) + rows_i).astype(F32) * inv[0:1, :]
        cosf[...] = jnp.cos(angle)
        sine = jnp.sin(angle)
        sinf[...] = jnp.where(cols_i < HD // 2, sine, -sine)
        for name in ("q", "do", "fo"):
            loads[name].wait()
        ones = jnp.ones((8, HD), BF16)
        for h in range(HQ):
            cols = slice(h * HD, (h + 1) * HD)
            prod = do[:, cols].astype(F32) * fo[:, cols].astype(F32)
            hi = prod.astype(BF16)
            lo = (prod - hi.astype(F32)).astype(BF16)
            delta[h : h + 1] = (nt(ones, hi) + nt(ones, lo))[0:1]

    def unrotate(grad):
        return grad * cosf[...] + pltpu.roll(grad, HD // 2, 1) * sinf[...]

    def attend(h, kk, vv, bb):
        a, b = slice(2 * h * HD, (2 * h + 1) * HD), slice((2 * h + 1) * HD, (2 * h + 2) * HD)
        qs = jnp.concatenate([q[:, a], q[:, b]], axis=0)
        dos = jnp.concatenate([do[:, a], do[:, b]], axis=0)
        lse_h = jnp.concatenate([lse[2 * h : 2 * h + 1], lse[2 * h + 1 : 2 * h + 2]], axis=1)
        delta_h = jnp.concatenate([delta[2 * h : 2 * h + 1], delta[2 * h + 1 : 2 * h + 2]], axis=1)
        capped = jnp.tanh(nt(kk, qs) * F32(1.0 / 600.0))
        prob = jnp.exp(F32(50.0) * capped - lse_h + jnp.concatenate([bb, bb], axis=1))
        dprob = nt(vv, dos)
        ds = (prob * (dprob - delta_h) * (F32(1.0 / 12.0) - F32(1.0 / 12.0) * (capped * capped))).astype(BF16)
        return tn(ds, kk), nn(ds, qs), nn(prob.astype(BF16), dos)

    def first(gi):
        for hh in range(2):
            h = gi * 2 + hh
            cols = slice(h * HD, (h + 1) * HD)
            kk = jnp.concatenate([k[:, cols], kvr[0, 0, :, cols]], axis=0)
            vv = jnp.concatenate([v[:, cols], kvr[0, 1, :, cols]], axis=0)
            dq, dk, dv = attend(h, kk, vv, bias[0:2].reshape(2 * TOK, TOK))
            dq_acc[h] = dq
            for j, val in enumerate((dk, dv)):
                home[gi, hh, j] = val[0:TOK]
                one_part[gi, hh, j] = val[TOK : 2 * TOK]

    def second(gi):
        for j in range(2):
            cps["two", gi, j].wait_recv()
            cps["pri", gi, j].wait_recv()
        for hh in range(2):
            h = gi * 2 + hh
            cols = slice(h * HD, (h + 1) * HD)
            kk = kvr[1:3, 0, :, cols].reshape(2 * TOK, HD)
            vv = kvr[1:3, 1, :, cols].reshape(2 * TOK, HD)
            dq, dk, dv = attend(h, kk, vv, bias[2:4].reshape(2 * TOK, TOK))
            for j, val in enumerate((dk, dv)):
                two_send[gi, hh, j] = val[0:TOK].astype(BF16)
                pri_send[gi, hh, j] = val[TOK : 2 * TOK].astype(BF16)
            total = dq_acc[h] + dq
            for i in range(2):
                at = (2 * h + i) * HD
                g[:, at : at + HD] = unrotate(total[i * TOK : (i + 1) * TOK]).astype(BF16)
        send(("ret", gi), two_send.at[gi], two_recv.at[gi], ret_s.at[1, gi], ret_r.at[1, gi], down)

    def carry(gi):
        cps["ret", gi].wait_recv()
        car_send[gi] = (two_recv[gi].astype(F32) + one_part[gi]).astype(BF16)
        send(("car", gi), car_send.at[gi], car_recv.at[gi], ret_s.at[2, gi], ret_r.at[2, gi], down)

    def settle(gi):
        cps["car", gi].wait_recv()
        cps["rpri", gi].wait_recv()
        for hh in range(2):
            h = gi * 2 + hh
            dk, dv = [
                home[gi, hh, j] + car_recv[gi, hh, j].astype(F32) + pri_recv[gi, hh, j].astype(F32)
                for j in range(2)
            ]
            at = HQ * HD + h * HD
            g[:, at : at + HD] = unrotate(dk).astype(BF16)
            at = (HQ + HK) * HD + h * HD
            g[:, at : at + HD] = dv.astype(BF16)

    def base(ch, who):
        lo, hi = CHUNKS[ch]
        return pl.ds(pl.multiple_of(lo + who * (hi - lo), HALF), HALF)

    def swap(ch):
        gq[ch, 0] = g[:, base(ch, c)]
        send(("g1", ch), g.at[:, base(ch, 1 - c)], gq.at[ch, 1], gx_s.at[ch, 0], gx_r.at[ch, 0], core)
        send(("g2", ch), gq.at[ch, 0], gq.at[ch, 2], gx_s.at[ch, 1], gx_r.at[ch, 1], far)
        if ch < GROUPS:
            send(
                ("rpri", ch), pri_send.at[ch], pri_recv.at[ch], ret_s.at[0, ch], ret_r.at[0, ch], prv
            )

    def relay(ch):
        cps["g1", ch].wait_recv()
        send(("g3", ch), gq.at[ch, 1], gq.at[ch, 3], gx_s.at[ch, 2], gx_r.at[ch, 2], far)

    def term(ch, chain, s):
        way, hops = CHAINS[ch][chain]
        return part[ch, (z + 2 * RING + way * (hops - s)) % RING]

    def hop(ch, chain, s, val):
        rs_send[ch, chain, s] = val.astype(BF16)
        send(
            ("rs", ch, chain, s), rs_send.at[ch, chain, s], rs_recv.at[ch, chain, s],
            rs_ss.at[ch, chain, s], rs_rs.at[ch, chain, s], up if CHAINS[ch][chain][0] > 0 else down,
        )

    def mult(ch):
        cps["g2", ch].wait_recv()
        cps["g3", ch].wait_recv()
        gs = gq[ch].reshape(QUAD * TOK, HALF)
        for piece in range(2):
            at = slice(piece * 4, piece * 4 + 4)
            xs = jnp.concatenate(
                [xt.at[:, xh][at], xt_core[at], xt_far[0, at], xt_far[1, at]], axis=-1
            ).reshape(4 * ROWS, QUAD * TOK)
            part[ch, at] = nn(xs, gs).reshape(4, ROWS, HALF)
        for chain in range(2):
            hop(ch, chain, 0, term(ch, chain, 0))

    def step(ch, s):
        for chain in range(2):
            if s < CHAINS[ch][chain][1]:
                cps["rs", ch, chain, s - 1].wait_recv()
                hop(ch, chain, s, rs_recv[ch, chain, s - 1].astype(F32) + term(ch, chain, s))

    def finish(ch):
        val = part[ch, z]
        for chain in range(2):
            end = CHAINS[ch][chain][1] - 1
            cps["rs", ch, chain, end].wait_recv()
            val = val + rs_recv[ch, chain, end].astype(F32)
        fin[ch, 0] = val[0 : ROWS // 2]
        fin[ch, 1] = val[ROWS // 2 :]
        fin_send[ch] = fin[ch, 1 - c].astype(BF16)
        send(("fin", ch), fin_send.at[ch], fin_recv.at[ch], fin_s.at[ch], fin_r.at[ch], core)
        wout[:, base(ch, c)] = fin[ch, c].astype(BF16)

    def last(ch):
        cps["fin", ch].wait_recv()
        wout[:, base(ch, 1 - c)] = fin_recv[ch]

    steps = {
        "one": one, "pri": pri, "fwd": fwd, "turn": turn, "prep": prep, "xon": xon, "xready": xready,
        "first": first, "second": second, "carry": carry, "settle": settle, "swap": swap, "relay": relay,
        "mult": mult, "step": step, "finish": finish, "last": last,
    }
    settled = 0
    for name, *which in ORDER:
        steps[name](*which)
        if name in ("second", "settle"):
            settled += 1
            if settled == 2 * GROUPS:
                store = pltpu.make_async_copy(g, gout, in_s.at[10])
                store.start()
    store.wait()
    for cp in sends:
        cp.wait_send()


def hand_over(qkv, weights, qkv_out, weights_out):
    qkv_out[...] = qkv[...]
    weights_out[...] = weights[...]


def local(hidden_in, queries, keys, values, fwd_out, out_grad, lse, block_order, doc_lengths):
    freq = 10000.0 ** (-2.0 * np.arange(HD // 2, dtype=np.float32) / HD)
    inv = jnp.asarray(np.broadcast_to(np.concatenate([freq, freq])[None, :], (8, HD)).astype(np.float32))
    vm = pl.BlockSpec(memory_space=pltpu.VMEM)
    sm = pl.BlockSpec(memory_space=pltpu.SMEM)
    hbm = pl.BlockSpec(memory_space=pl.ANY)
    ret = pltpu.VMEM((GROUPS, 2, 2, TOK, HD), BF16)
    dma = pltpu.SemaphoreType.DMA
    nch = len(CHUNKS)
    qkv, weights = pl.pallas_call(
        kernel,
        out_shape=(
            jax.ShapeDtypeStruct((TOK, COLS), BF16),
            jax.ShapeDtypeStruct((ROWS // 2, COLS), BF16),
        ),
        in_specs=[hbm] * 10,
        out_specs=(hbm, vm),
        scratch_shapes=[
            pltpu.VMEM((TOK, D), BF16),
            pltpu.VMEM((TOK, HQ * HD), BF16),
            pltpu.VMEM((TOK, HK * HD), BF16),
            pltpu.VMEM((TOK, HK * HD), BF16),
            pltpu.VMEM((TOK, HQ * HD), BF16),
            pltpu.VMEM((TOK, HQ * HD), BF16),
            pltpu.VMEM((HQ, TOK), F32),
            pltpu.VMEM((8, HD), F32),
            pltpu.SMEM((64,), jnp.int32),
            pltpu.SMEM((1, 4), jnp.int32),
            pltpu.VMEM((3, 2, TOK, HK * HD), BF16),
            pltpu.VMEM((4, TOK, TOK), F32),
            pltpu.VMEM((TOK, HD), F32),
            pltpu.VMEM((TOK, HD), F32),
            pltpu.VMEM((HQ, TOK), F32),
            pltpu.VMEM((HK, 2 * TOK, HD), F32),
            pltpu.VMEM((GROUPS, 2, 2, TOK, HD), F32),
            pltpu.VMEM((GROUPS, 2, 2, TOK, HD), F32),
            ret, ret, ret, ret, ret, ret,
            pltpu.VMEM((TOK, COLS), BF16),
            pltpu.VMEM((RING, 2, ROWS, TOK), BF16),
            pltpu.VMEM((RING, ROWS, TOK), BF16),
            pltpu.VMEM((2, RING, ROWS, TOK), BF16),
            pltpu.VMEM((nch, QUAD, TOK, HALF), BF16),
            pltpu.VMEM((nch, RING, ROWS, HALF), F32),
            pltpu.VMEM((nch, 2, 4, ROWS, HALF), BF16),
            pltpu.VMEM((nch, 2, 4, ROWS, HALF), BF16),
            pltpu.VMEM((nch, 2, ROWS // 2, HALF), F32),
            pltpu.VMEM((nch, ROWS // 2, HALF), BF16),
            pltpu.VMEM((nch, ROWS // 2, HALF), BF16),
            dma((11,)),
            dma((3, GROUPS, 2)), dma((3, GROUPS, 2)),
            dma((3, GROUPS)), dma((3, GROUPS)),
            dma((3,)), dma((3,)),
            dma((nch, 3)), dma((nch, 3)),
            dma((nch, 2, 4)), dma((nch, 2, 4)),
            dma((nch,)), dma((nch,)),
        ],
        compiler_params=pltpu.CompilerParams(
            collective_id=0, has_side_effects=True, vmem_limit_bytes=58 * 1024 * 1024
        ),
        cost_estimate=pl.CostEstimate(flops=4 * 10**9, bytes_accessed=6 * 10**6, transcendentals=2 * 10**6),
    )(
        hidden_in[0], queries[0], keys[0], values[0], fwd_out[0], out_grad[0], lse[0],
        block_order, doc_lengths, inv,
    )
    pieces = 2
    blocks = [pl.BlockSpec((TOK, COLS // pieces), lambda i: (0, i)), pl.BlockSpec((ROWS // 2, COLS // pieces), lambda i: (0, i))]
    qkv, weights = pl.pallas_call(
        hand_over,
        out_shape=(
            jax.ShapeDtypeStruct((TOK, COLS), BF16),
            jax.ShapeDtypeStruct((ROWS // 2, COLS), BF16),
        ),
        grid=(pieces,),
        in_specs=blocks,
        out_specs=blocks,
    )(qkv, weights)
    return (qkv[None], weights[None])


def solution(mesh):
    tokens = P("fsdp", ("outer", "inner"), None)
    in_specs = (tokens,) * 6 + (P("fsdp", None, ("outer", "inner")), P(), P("fsdp", None))
    out_specs = (tokens, P("outer", ("inner", "fsdp"), None))
    return jax.shard_map(local, mesh=mesh, in_specs=in_specs, out_specs=out_specs, check_vma=False)
```
